32 devices in a mesh: grp: 2 (over x), src: 2 (over core), lat: 8 (over z, y).
Axes of the slice: x: 2, y: 2, z: 4, core: 2. Of those that a mesh axis runs over, the one named last changes fastest.
Arguments:
- store: bfloat16 [256, 2, 4096], P(('grp', 'lat'), 'src'), parts along dimension 0, may hold values from -6.4 to 6.4
- row_index: int32 [128], P(('grp', 'lat')), parts along dimension 0, may hold values from 0 to 15
- w_enc: bfloat16 [4, 4096, 1024], P(('grp', 'src'), None, 'lat'), parts along dimension 0, may hold values from -0.0625 to 0.0625
- decoder_matrix: bfloat16 [4, 1024, 4096], P(('grp', 'src'), 'lat'), parts along dimension 0, may hold values from -0.46875 to 0.46875
- m_enc: bfloat16 [4, 4096, 1024], P(('grp', 'src'), None, 'lat'), parts along dimension 0, may hold values from -0.0001235962 to 0.0001235962
- v_enc: bfloat16 [4, 4096, 1024], P(('grp', 'src'), None, 'lat'), parts along dimension 0, may hold values from 1.16415322e-13 to 1.4202669e-09
- m_dec: bfloat16 [4, 1024, 4096], P(('grp', 'src'), 'lat'), parts along dimension 0, may hold values from -0.0001235962 to 0.0001235962
- v_dec: bfloat16 [4, 1024, 4096], P(('grp', 'src'), 'lat'), parts along dimension 0, may hold values from 1.16415322e-13 to 1.4202669e-09
Outputs:
- encoder_step: bfloat16 [4, 4096, 1024], P(('grp', 'src'), None, 'lat'), parts along dimension 0
- decoder_step: bfloat16 [4, 1024, 4096], P(('grp', 'src'), 'lat'), parts along dimension 0
The draws below stay inside these ranges and needn't reach their ends.
There are 2 independent parts, one for each index of `grp`. The reference program is written for one: setup_inputs(seed, part) draws one part's arguments, and reference() takes and returns one part's arrays. A program takes and returns all parts, laid end to end along the dimension named above; each array names one. Nothing has to cross between parts.
All inputs are finite; a program needn't handle non-finite values.
Results may differ from the reference program's by a relative error of at most 0.009.
Values may be sent and summed in bfloat16 or wider, within the bound.
No kernel may reach another device: no remote copies, remote signals or barrier semaphores. Data moves between devices by JAX's collectives and lax.ppermute only.
A program may use at most 128 MiB of HBM per device.

```python
import jax
import jax.numpy as jnp
from jax import lax

D = 4096
LAT_ROWS = 8
STORE_DEV = 16
S = 2
L = 1024
B = 64
ROWS = 128


def grad_scale():
    return 2.0 / (S * D * B ** 0.5)


def second_moment(key, lat_axis):
    key_rows = jax.random.fold_in(key, 1)
    key_cells = jax.random.fold_in(key, 2)
    if lat_axis == 2:
        shape = (S, D, L)
        ramp = (jnp.arange(L, dtype=jnp.float32) / max(L - 1, 1))[None, None, :]
        rows = jax.random.uniform(key_rows, (D,), jnp.float32)[None, :, None]
    else:
        shape = (S, L, D)
        ramp = (jnp.arange(L, dtype=jnp.float32) / max(L - 1, 1))[None, :, None]
        rows = jax.random.uniform(key_rows, (D,), jnp.float32)[None, None, :]
    cells = 0.5 + jax.random.uniform(key_cells, shape, jnp.float32)
    source = (3.0 ** (-jnp.arange(S, dtype=jnp.float32) / max(S - 1, 1)))[:, None, None]
    level = grad_scale() ** 2
    return level * 10.0 ** (-(ramp + rows)) * cells * source


def draw_store(key, part):
    key = jax.random.fold_in(key, 3)
    key_base = jax.random.fold_in(key, 0)
    ramp = 10.0 ** (0.5 * jnp.arange(ROWS, dtype=jnp.float32) / max(ROWS - 1, 1)) / 2.0
    base = jnp.clip(jax.random.normal(key_base, (ROWS, S, D), jnp.float32), -4.0, 4.0)
    values = base * ramp[:, None, None]
    return values.astype(jnp.bfloat16)


def draw_decoder_matrix(key, part):
    key = jax.random.fold_in(key, 5)
    key_base, key_lat, key_feat = jax.random.split(key, 3)
    base = jnp.clip(jax.random.normal(key_base, (S, L, D), jnp.float32), -4.0, 4.0)
    lat_factor = 10.0 ** (0.5 * jax.random.uniform(key_lat, (L,), jnp.float32)) / 2.0
    feat_factor = 10.0 ** (0.5 * jax.random.uniform(key_feat, (D,), jnp.float32)) / 2.0
    source = 0.5 + jnp.arange(S, dtype=jnp.float32) / max(S - 1, 1)
    values = base * source[:, None, None] * lat_factor[None, :, None] * feat_factor[None, None, :]
    return (values / L ** 0.5).astype(jnp.bfloat16)


def draw_m_enc(key, part):
    key = jax.random.fold_in(key, 7)
    base = jnp.clip(jax.random.normal(key, (S, D, L), jnp.float32), -4.0, 4.0)
    return (base * grad_scale()).astype(jnp.bfloat16)


def draw_m_dec(key, part):
    key = jax.random.fold_in(key, 9)
    base = jnp.clip(jax.random.normal(key, (S, L, D), jnp.float32), -4.0, 4.0)
    return (base * grad_scale()).astype(jnp.bfloat16)


def draw_v_enc(key, part):
    key = jax.random.fold_in(key, 13)
    return second_moment(key, 2).astype(jnp.bfloat16)


def draw_v_dec(key, part):
    key = jax.random.fold_in(key, 17)
    return second_moment(key, 1).astype(jnp.bfloat16)


def plant(result, own_key, smallest, high):
    shape = result.shape
    index_at = [jax.random.randint(jax.random.fold_in(own_key, axis), (), 0, shape[axis]) for axis in range(len(shape))]
    result = result.at[tuple(index_at)].set(smallest)
    longest = shape.index(max(shape))
    index_at[longest] = (index_at[longest] + 1) % shape[longest]
    return result.at[tuple(index_at)].set(high)


def block_scale(stream_key, dims, pieces, low, top_value):
    level = 1.0
    for axis_at, blocks in pieces:
        heights = jax.random.uniform(jax.random.fold_in(jax.random.fold_in(stream_key, 6), axis_at), (blocks,), jnp.float32, low / len(pieces), top_value / len(pieces))
        level = level * jnp.repeat(jnp.exp(heights), dims[axis_at] // blocks).reshape((-1,) + (1,) * (len(dims) - 1 - axis_at))
    return level


def noise(own_key, extent, scale, most, cuts=(), kind=jnp.bfloat16):
    array = jax.random.normal(own_key, extent, jnp.float32) * scale
    if len(cuts) > 0:
        array = block_scale(own_key, extent, cuts, -0.22, 0.18) * array
    return jnp.clip(array, min=-most, max=most).astype(kind)


def setup_inputs(seed: int = 0, part: int = 0) -> dict:
    seeds = jax.random.split(jax.random.key(seed), 9)
    part_keys = jax.random.split(jax.random.fold_in(seeds[8], part), 9)
    return {
        "store": draw_store(jax.random.fold_in(jax.random.fold_in(seeds[8], part), 71), part),
        "row_index": plant(jax.random.randint(part_keys[1], (B,), 0, STORE_DEV), jax.random.fold_in(part_keys[1], 1), 0, STORE_DEV - 1).astype(jnp.int32),
        "w_enc": noise(part_keys[2], (S, D, L), (S * D) ** -0.5, 0.0625, ((0, 2), (2, 8))),
        "decoder_matrix": draw_decoder_matrix(jax.random.fold_in(jax.random.fold_in(seeds[8], part), 71), part),
        "m_enc": draw_m_enc(jax.random.fold_in(jax.random.fold_in(seeds[8], part), 71), part),
        "v_enc": draw_v_enc(jax.random.fold_in(jax.random.fold_in(seeds[8], part), 71), part),
        "m_dec": draw_m_dec(jax.random.fold_in(jax.random.fold_in(seeds[8], part), 71), part),
        "v_dec": draw_v_dec(jax.random.fold_in(jax.random.fold_in(seeds[8], part), 71), part),
    }


sparsity = 0.5
beta_one = 0.9
beta_two = 0.95
adam_eps = 1e-08
clip_rms = 1.0
norm_eps = 1e-06

def adam_direction(gradient, moment_one, moment_two):
    first_wide = moment_one.astype(jnp.float32)
    second_wide = moment_two.astype(jnp.float32)
    new_first = beta_one * first_wide + (1.0 - beta_one) * gradient
    new_second = beta_two * second_wide + (1.0 - beta_two) * gradient * gradient
    return new_first / (jnp.sqrt(new_second) + adam_eps)

def reference(store, row_index, w_enc, decoder_matrix, m_enc, v_enc, m_dec, v_dec):
    upper_bound = lax.Precision.HIGHEST
    row_ids = jnp.arange(B, dtype=jnp.int32) // LAT_ROWS * STORE_DEV + row_index.astype(jnp.int32)
    batch_rows = store[row_ids]
    batch_wide = batch_rows.astype(jnp.float32)
    enc_wide = w_enc.astype(jnp.float32)
    wide_decoder_weight = decoder_matrix.astype(jnp.float32)
    preact = jnp.einsum('bsd,sdl->bl', batch_wide, enc_wide, precision=upper_bound)
    feature_codes = jnp.maximum(preact, 0.0).astype(jnp.bfloat16)
    wide_latent_codes = feature_codes.astype(jnp.float32)
    dec_norm = jnp.sqrt(lax.optimization_barrier(jnp.sum(wide_decoder_weight * wide_decoder_weight, axis=2)) + norm_eps)
    norm_total = lax.optimization_barrier(jnp.sum(dec_norm, axis=0))
    rebuilt_output = jnp.einsum('ip,xpt->ixt', wide_latent_codes, wide_decoder_weight, precision=upper_bound)
    residual_error_rows = (rebuilt_output - batch_wide).astype(jnp.bfloat16)
    wide_residual_error = residual_error_rows.astype(jnp.float32)
    element_count = float(B * S * D)
    squared_error_scale = 2.0 / element_count
    sparse_scale = sparsity / element_count
    column_sums = lax.optimization_barrier(jnp.sum(wide_latent_codes, axis=0))
    decoder_gradient = squared_error_scale * jnp.einsum('yt,ygh->gth', wide_latent_codes, wide_residual_error, precision=upper_bound)
    decoder_gradient = decoder_gradient + sparse_scale * column_sums[None, :, None] * wide_decoder_weight / dec_norm[:, :, None]
    latent_code_gradient = jnp.einsum('jva,vfa->jf', wide_residual_error, wide_decoder_weight, precision=upper_bound)
    pre_grad = jnp.where(preact > 0, squared_error_scale * latent_code_gradient + sparse_scale * norm_total[None, :], 0.0)
    pre_grad = pre_grad.astype(jnp.bfloat16).astype(jnp.float32)
    grad_enc = jnp.einsum('bsd,bl->sdl', batch_wide, pre_grad, precision=upper_bound)
    enc_dir = adam_direction(grad_enc, m_enc, v_enc)
    dec_dir = adam_direction(decoder_gradient, m_dec, v_dec)
    squares = jnp.sum(enc_dir * enc_dir) + jnp.sum(dec_dir * dec_dir)
    update_rms = jnp.sqrt(squares / float(2 * S * D * L))
    factor = 1.0 / jnp.maximum(1.0, update_rms / clip_rms)
    return ((enc_dir * factor).astype(jnp.bfloat16), (dec_dir * factor).astype(jnp.bfloat16))
```

```python
import jax
import jax.numpy as jnp
from jax import lax
from jax.sharding import PartitionSpec as P

sparsity = 0.5
beta_one = 0.9
beta_two = 0.95
adam_eps = 1e-08
clip_rms = 1.0
norm_eps = 1e-06
f32 = jnp.float32
bf16 = jnp.bfloat16


def swap(value, axis, bits):
    count = lax.axis_size(axis)
    return lax.ppermute(value, axis, [(i, i ^ bits) for i in range(count)])


def adam_direction(gradient, moment_one, moment_two):
    first_wide = moment_one.astype(f32)
    second_wide = moment_two.astype(f32)
    new_first = beta_one * first_wide + (1.0 - beta_one) * gradient
    new_second = beta_two * second_wide + (1.0 - beta_two) * gradient * gradient
    return new_first / (jnp.sqrt(new_second) + adam_eps)


def pack(value):
    top = jnp.max(jnp.abs(value), axis=-1, keepdims=True)
    level = jnp.ceil(16.0 * jnp.log2(jnp.maximum(top, 1e-30)))
    scaled = jnp.round(value * (32767.0 * jnp.exp2(level * -0.0625)))
    scaled = jnp.clip(scaled, -32767.0, 32767.0)
    level = jnp.broadcast_to(level, value.shape[:-1] + (128,))
    return jnp.concatenate([scaled, level], axis=-1).astype(jnp.int16)


def unpack(packed):
    wide = packed.astype(f32)
    return wide[..., :-128] * (jnp.exp2(wide[..., -128:-127] * 0.0625) * (1.0 / 32767.0))


def quad_gather(quarter):
    return [quarter] + [swap(quarter, "lat", k) for k in (1, 2, 3)]


def body(store, row_index, w_enc, decoder_matrix, m_enc, v_enc, m_dec, v_dec):
    lat_count = lax.axis_size("lat")
    high_bits = [4 << i for i in range((lat_count // 4).bit_length() - 1)]
    store = store[:, 0, :]
    w_enc, decoder_matrix, m_enc, v_enc, m_dec, v_dec = (
        a[0] for a in (w_enc, decoder_matrix, m_enc, v_enc, m_dec, v_dec)
    )
    features, latents = w_enc.shape
    own_count = row_index.shape[0]
    batch_count = own_count * lat_count
    source_count = lax.axis_size("src")
    element_count = float(batch_count * source_count * features)
    squared_error_scale = 2.0 / element_count
    sparse_scale = sparsity / element_count

    pick = row_index[:, None] == jnp.arange(store.shape[0], dtype=row_index.dtype)[None, :]
    own_rows = jnp.dot(pick.astype(bf16), store, preferred_element_type=f32).astype(bf16)
    quarter = own_rows
    for bit in high_bits:
        quarter = jnp.concatenate([quarter, swap(quarter, "lat", bit)])
    quarter_count = quarter.shape[0]
    batch_rows = jnp.concatenate(quad_gather(quarter))

    partial_value = jnp.dot(batch_rows, w_enc, preferred_element_type=f32)
    dec_wide = decoder_matrix.astype(f32)
    dec_norm = jnp.sqrt(jnp.sum(dec_wide * dec_wide, axis=1) + norm_eps)
    preact = partial_value + swap(partial_value, "src", 1)
    norm_total = dec_norm + swap(dec_norm, "src", 1)
    feature_codes = jnp.maximum(preact, 0.0).astype(bf16)
    parts = jnp.dot(feature_codes, decoder_matrix, preferred_element_type=f32)
    parts = parts.reshape(4, quarter_count, features)
    total = parts[0]
    for k in (1, 2, 3):
        total = total + unpack(swap(pack(parts[k]), "lat", k))
    for at, bit in enumerate(high_bits):
        other = unpack(swap(pack(total), "lat", bit))
        span = own_count << at
        other = jnp.flip(other.reshape(-1, 2, span, features), 1).reshape(quarter_count, features)
        total = total + other
    quarter_error = (total - quarter.astype(f32)).astype(bf16)
    error_rows = jnp.concatenate(quad_gather(quarter_error))

    column_sums = jnp.sum(feature_codes.astype(f32), axis=0)
    decoder_gradient = squared_error_scale * lax.dot_general(
        feature_codes, error_rows, (((0,), (0,)), ((), ())), preferred_element_type=f32
    )
    decoder_gradient = decoder_gradient + (sparse_scale * column_sums / dec_norm)[:, None] * dec_wide
    dec_dir = adam_direction(decoder_gradient, m_dec, v_dec)
    partial_back = lax.dot_general(
        error_rows, decoder_matrix, (((1,), (1,)), ((), ())), preferred_element_type=f32
    )
    back = partial_back + swap(partial_back, "src", 1)
    pre_grad = jnp.where(
        preact > 0, squared_error_scale * back + sparse_scale * norm_total[None, :], 0.0
    ).astype(bf16)
    grad_enc = lax.dot_general(
        batch_rows, pre_grad, (((0,), (0,)), ((), ())), preferred_element_type=f32
    )
    enc_dir = adam_direction(grad_enc, m_enc, v_enc)
    squares = jnp.sum(enc_dir * enc_dir) + jnp.sum(dec_dir * dec_dir)
    squares = squares.reshape(1, 1)
    squares = squares + swap(squares, "src", 1)
    bit = 1
    while bit < lat_count:
        squares = squares + swap(squares, "lat", bit)
        bit *= 2
    update_rms = jnp.sqrt(squares / float(2 * source_count * features * latents * lat_count))
    factor = 1.0 / jnp.maximum(1.0, update_rms / clip_rms)
    return ((enc_dir * factor).astype(bf16)[None], (dec_dir * factor).astype(bf16)[None])


def solution(mesh):
    return jax.shard_map(
        body,
        mesh=mesh,
        in_specs=(
            P(("grp", "lat"), "src", None),
            P(("grp", "lat")),
            P(("grp", "src"), None, "lat"),
            P(("grp", "src"), "lat", None),
            P(("grp", "src"), None, "lat"),
            P(("grp", "src"), None, "lat"),
            P(("grp", "src"), "lat", None),
            P(("grp", "src"), "lat", None),
        ),
        out_specs=(P(("grp", "src"), None, "lat"), P(("grp", "src"), "lat", None)),
        check_vma=False,
    )
```

```python
import jax
import jax.numpy as jnp
from jax import lax
from jax.sharding import PartitionSpec as P

sparsity = 0.5
beta_one = 0.9
beta_two = 0.95
adam_eps = 1e-08
clip_rms = 1.0
norm_eps = 1e-06
f32 = jnp.float32
bf16 = jnp.bfloat16


def swap(value, axis, bits):
    count = lax.axis_size(axis)
    return lax.ppermute(value, axis, [(i, i ^ bits) for i in range(count)])


def adam_direction(gradient, moment_one, moment_two):
    first_wide = moment_one.astype(f32)
    second_wide = moment_two.astype(f32)
    new_first = beta_one * first_wide + (1.0 - beta_one) * gradient
    new_second = beta_two * second_wide + (1.0 - beta_two) * gradient * gradient
    size = new_second * lax.rsqrt(new_second) + adam_eps
    return new_first * lax.rsqrt(size * size)


def pack(value):
    top = jnp.max(jnp.abs(value), axis=-1, keepdims=True)
    level = jnp.ceil(16.0 * jnp.log2(jnp.maximum(top, 1e-30)))
    scaled = jnp.round(value * (32766.0 * jnp.exp2(level * -0.0625)))
    scaled = jnp.clip(scaled, -32766.0, 32766.0).astype(jnp.int32)
    column = lax.broadcasted_iota(jnp.int32, value.shape, value.ndim - 1)
    code = level.astype(jnp.int32) + 4096
    bit = (code >> jnp.minimum(column, 15)) & 1
    return jnp.where(column < 16, (scaled & -2) | bit, scaled).astype(jnp.int16)


def unpack(packed):
    head = packed[..., :128].astype(jnp.int32) & 1
    column = lax.broadcasted_iota(jnp.int32, head.shape, head.ndim - 1)
    code = jnp.sum(jnp.where(column < 16, head << jnp.minimum(column, 15), 0), axis=-1, keepdims=True)
    step = jnp.exp2((code - 4096).astype(f32) * 0.0625) * (1.0 / 32766.0)
    return packed.astype(f32) * step


def quad_gather(quarter):
    return [quarter] + [swap(quarter, "lat", k) for k in (1, 2, 3)]


def body(store, row_index, w_enc, decoder_matrix, m_enc, v_enc, m_dec, v_dec):
    lat_count = lax.axis_size("lat")
    high_bits = [4 << i for i in range((lat_count // 4).bit_length() - 1)]
    store = store[:, 0, :]
    w_enc, decoder_matrix, m_enc, v_enc, m_dec, v_dec = (
        a[0] for a in (w_enc, decoder_matrix, m_enc, v_enc, m_dec, v_dec)
    )
    features, latents = w_enc.shape
    own_count = row_index.shape[0]
    batch_count = own_count * lat_count
    source_count = lax.axis_size("src")
    element_count = float(batch_count * source_count * features)
    squared_error_scale = 2.0 / element_count
    sparse_scale = sparsity / element_count

    pick = row_index[:, None] == jnp.arange(store.shape[0], dtype=row_index.dtype)[None, :]
    own_rows = jnp.dot(pick.astype(bf16), store, preferred_element_type=f32).astype(bf16)
    quarter = own_rows
    for bit in high_bits:
        quarter = jnp.concatenate([quarter, swap(quarter, "lat", bit)])
    quarter_count = quarter.shape[0]
    batch_rows = jnp.concatenate(quad_gather(quarter))

    partial_value = jnp.dot(batch_rows, w_enc, preferred_element_type=f32)
    dec_wide = decoder_matrix.astype(f32)
    dec_norm = jnp.sqrt(jnp.sum(dec_wide * dec_wide, axis=1) + norm_eps)
    preact = partial_value + swap(partial_value, "src", 1)
    norm_total = dec_norm + swap(dec_norm, "src", 1)
    feature_codes = jnp.maximum(preact, 0.0).astype(bf16)
    parts = jnp.dot(feature_codes, decoder_matrix, preferred_element_type=f32)
    parts = parts.reshape(4, quarter_count, features)
    total = parts[0]
    for k in (1, 2, 3):
        total = total + unpack(swap(pack(parts[k]), "lat", k))
    for at, bit in enumerate(high_bits):
        other = unpack(swap(pack(total), "lat", bit))
        span = own_count << at
        other = jnp.flip(other.reshape(-1, 2, span, features), 1).reshape(quarter_count, features)
        total = total + other
    quarter_error = (total - quarter.astype(f32)).astype(bf16)
    error_rows = jnp.concatenate(quad_gather(quarter_error))

    column_sums = jnp.sum(feature_codes.astype(f32), axis=0)
    decoder_gradient = squared_error_scale * lax.dot_general(
        feature_codes, error_rows, (((0,), (0,)), ((), ())), preferred_element_type=f32
    )
    decoder_gradient = decoder_gradient + (sparse_scale * column_sums / dec_norm)[:, None] * dec_wide
    dec_dir = adam_direction(decoder_gradient, m_dec, v_dec)
    partial_back = lax.dot_general(
        error_rows, decoder_matrix, (((1,), (1,)), ((), ())), preferred_element_type=f32
    )
    back = partial_back + swap(partial_back, "src", 1)
    pre_grad = jnp.where(
        preact > 0, squared_error_scale * back + sparse_scale * norm_total[None, :], 0.0
    ).astype(bf16)
    grad_enc = lax.dot_general(
        batch_rows, pre_grad, (((0,), (0,)), ((), ())), preferred_element_type=f32
    )
    enc_dir = adam_direction(grad_enc, m_enc, v_enc)
    squares = jnp.sum((enc_dir * enc_dir).reshape(-1, 8, 128), axis=0)
    squares = squares + jnp.sum((dec_dir * dec_dir).reshape(latents // 8, 8, -1, 128), axis=(0, 2))
    squares = squares + swap(squares, "src", 1)
    bit = 1
    while bit < lat_count:
        squares = squares + swap(squares, "lat", bit)
        bit *= 2
    squares = jnp.sum(squares)
    update_rms = jnp.sqrt(squares / float(2 * source_count * features * latents * lat_count))
    factor = 1.0 / jnp.maximum(1.0, update_rms / clip_rms)
    return ((enc_dir * factor).astype(bf16)[None], (dec_dir * factor).astype(bf16)[None])


def solution(mesh):
    return jax.shard_map(
        body,
        mesh=mesh,
        in_specs=(
            P(("grp", "lat"), "src", None),
            P(("grp", "lat")),
            P(("grp", "src"), None, "lat"),
            P(("grp", "src"), "lat", None),
            P(("grp", "src"), None, "lat"),
            P(("grp", "src"), None, "lat"),
            P(("grp", "src"), "lat", None),
            P(("grp", "src"), "lat", None),
        ),
        out_specs=(P(("grp", "src"), None, "lat"), P(("grp", "src"), "lat", None)),
        check_vma=False,
    )
```

```python
import functools

import jax
import jax.numpy as jnp
from jax import lax
from jax.experimental import pallas as pl
from jax.experimental.pallas import tpu as pltpu
from jax.sharding import PartitionSpec as P

sparsity = 0.5
beta_one = 0.9
beta_two = 0.95
adam_eps = 1e-08
clip_rms = 1.0
norm_eps = 1e-06
f32 = jnp.float32
bf16 = jnp.bfloat16


def swap(value, axis, bits):
    count = lax.axis_size(axis)
    return lax.ppermute(value, axis, [(i, i ^ bits) for i in range(count)])


def adam_direction(gradient, first_part, second_part):
    new_first = first_part + (1.0 - beta_one) * gradient
    new_second = second_part + (1.0 - beta_two) * gradient * gradient
    size = new_second * lax.rsqrt(new_second) + adam_eps
    return new_first * lax.rsqrt(size * size)


def scale_kernel(count, squares_ref, enc_ref, dec_ref, enc_out, dec_out, enc_buf, dec_buf, sems):
    total = jnp.sum(squares_ref[...], keepdims=True)
    update_rms = jnp.sqrt(total / count)
    factor = 1.0 / jnp.maximum(1.0, update_rms / clip_rms)
    steps = 4
    copies = []
    for i in range(steps):
        for j, (src, buf, out) in enumerate(((enc_ref, enc_buf, enc_out), (dec_ref, dec_buf, dec_out))):
            rows = src.shape[0] // steps
            part = pl.ds(i * rows, rows)
            buf[part, :] = (src[part, :] * factor).astype(bf16)
            copy = pltpu.make_async_copy(buf.at[part, :], out.at[part, :], sems.at[i, j])
            copy.start()
            copies.append(copy)
    for copy in copies:
        copy.wait()


def scale(squares, enc_dir, dec_dir, count):
    return pl.pallas_call(
        functools.partial(scale_kernel, count),
        out_shape=(jax.ShapeDtypeStruct(enc_dir.shape, bf16), jax.ShapeDtypeStruct(dec_dir.shape, bf16)),
        in_specs=[pl.BlockSpec(memory_space=pltpu.VMEM)] * 3,
        out_specs=[pl.BlockSpec(memory_space=pl.ANY)] * 2,
        scratch_shapes=[
            pltpu.VMEM(enc_dir.shape, bf16),
            pltpu.VMEM(dec_dir.shape, bf16),
            pltpu.SemaphoreType.DMA((4, 2)),
        ],
        compiler_params=pltpu.CompilerParams(vmem_limit_bytes=24 << 20),
        name="scale_directions",
    )(squares, enc_dir, dec_dir)


def pack(value):
    top = jnp.max(jnp.abs(value), axis=-1, keepdims=True)
    level = jnp.ceil(16.0 * jnp.log2(jnp.maximum(top, 1e-30)))
    scaled = jnp.round(value * (32766.0 * jnp.exp2(level * -0.0625)))
    scaled = jnp.clip(scaled, -32766.0, 32766.0).astype(jnp.int32)
    column = lax.broadcasted_iota(jnp.int32, value.shape, value.ndim - 1)
    code = level.astype(jnp.int32) + 4096
    bit = (code >> jnp.minimum(column, 15)) & 1
    return jnp.where(column < 16, (scaled & -2) | bit, scaled).astype(jnp.int16)


def unpack(packed):
    head = packed[..., :128].astype(jnp.int32) & 1
    column = lax.broadcasted_iota(jnp.int32, head.shape, head.ndim - 1)
    code = jnp.sum(jnp.where(column < 16, head << jnp.minimum(column, 15), 0), axis=-1, keepdims=True)
    step = jnp.exp2((code - 4096).astype(f32) * 0.0625) * (1.0 / 32766.0)
    return packed.astype(f32) * step


def quad_gather(quarter):
    return [quarter] + [swap(quarter, "lat", k) for k in (1, 2, 3)]


def body(store, row_index, w_enc, decoder_matrix, m_enc, v_enc, m_dec, v_dec):
    lat_count = lax.axis_size("lat")
    high_bits = [4 << i for i in range((lat_count // 4).bit_length() - 1)]
    store = store[:, 0, :]
    w_enc, decoder_matrix, m_enc, v_enc, m_dec, v_dec = (
        a[0] for a in (w_enc, decoder_matrix, m_enc, v_enc, m_dec, v_dec)
    )
    features, latents = w_enc.shape
    own_count = row_index.shape[0]
    batch_count = own_count * lat_count
    source_count = lax.axis_size("src")
    element_count = float(batch_count * source_count * features)
    squared_error_scale = 2.0 / element_count
    sparse_scale = sparsity / element_count

    pick = row_index[:, None] == jnp.arange(store.shape[0], dtype=row_index.dtype)[None, :]
    own_rows = jnp.dot(pick.astype(bf16), store, preferred_element_type=f32).astype(bf16)
    quarter = own_rows
    for bit in high_bits:
        quarter = jnp.concatenate([quarter, swap(quarter, "lat", bit)])
    quarter_count = quarter.shape[0]
    batch_rows = jnp.concatenate(quad_gather(quarter))
    batch_rows, m_enc, v_enc, m_dec, v_dec = lax.optimization_barrier(
        (
            batch_rows,
            beta_one * m_enc.astype(f32),
            beta_two * v_enc.astype(f32),
            beta_one * m_dec.astype(f32),
            beta_two * v_dec.astype(f32),
        )
    )

    partial_value = jnp.dot(batch_rows, w_enc, preferred_element_type=f32)
    dec_wide = decoder_matrix.astype(f32)
    dec_norm = jnp.sqrt(jnp.sum(dec_wide * dec_wide, axis=1) + norm_eps)
    preact = partial_value + swap(partial_value, "src", 1)
    norm_total = dec_norm + swap(dec_norm, "src", 1)
    feature_codes = jnp.maximum(preact, 0.0).astype(bf16)
    parts = jnp.dot(feature_codes, decoder_matrix, preferred_element_type=f32)
    parts = parts.reshape(4, quarter_count, features)
    total = parts[0]
    for k in (1, 2, 3):
        total = total + unpack(swap(pack(parts[k]), "lat", k))
    for at, bit in enumerate(high_bits):
        other = unpack(swap(pack(total), "lat", bit))
        span = own_count << at
        other = jnp.flip(other.reshape(-1, 2, span, features), 1).reshape(quarter_count, features)
        total = total + other
    quarter_error = (total - quarter.astype(f32)).astype(bf16)
    error_rows = jnp.concatenate(quad_gather(quarter_error))

    column_sums = jnp.sum(feature_codes.astype(f32), axis=0)
    decoder_gradient = squared_error_scale * lax.dot_general(
        feature_codes, error_rows, (((0,), (0,)), ((), ())), preferred_element_type=f32
    )
    decoder_gradient = decoder_gradient + (sparse_scale * column_sums / dec_norm)[:, None] * dec_wide
    dec_dir = adam_direction(decoder_gradient, m_dec, v_dec)
    partial_back = lax.dot_general(
        error_rows, decoder_matrix, (((1,), (1,)), ((), ())), preferred_element_type=f32
    )
    back = partial_back + swap(partial_back, "src", 1)
    pre_grad = jnp.where(
        preact > 0, squared_error_scale * back + sparse_scale * norm_total[None, :], 0.0
    ).astype(bf16)
    grad_enc = lax.dot_general(
        batch_rows, pre_grad, (((0,), (0,)), ((), ())), preferred_element_type=f32
    )
    enc_dir = adam_direction(grad_enc, m_enc, v_enc)
    squares = jnp.sum((enc_dir * enc_dir).reshape(-1, 8, 128), axis=0)
    squares = squares + jnp.sum((dec_dir * dec_dir).reshape(latents // 8, 8, -1, 128), axis=(0, 2))
    squares = squares + swap(squares, "src", 1)
    bit = 1
    while bit < lat_count:
        squares = squares + swap(squares, "lat", bit)
        bit *= 2
    enc_step, dec_step = scale(
        squares, enc_dir, dec_dir, float(2 * source_count * features * latents * lat_count)
    )
    return enc_step[None], dec_step[None]


def solution(mesh):
    return jax.shard_map(
        body,
        mesh=mesh,
        in_specs=(
            P(("grp", "lat"), "src", None),
            P(("grp", "lat")),
            P(("grp", "src"), None, "lat"),
            P(("grp", "src"), "lat", None),
            P(("grp", "src"), None, "lat"),
            P(("grp", "src"), None, "lat"),
            P(("grp", "src"), "lat", None),
            P(("grp", "src"), "lat", None),
        ),
        out_specs=(P(("grp", "src"), None, "lat"), P(("grp", "src"), "lat", None)),
        check_vma=False,
    )
```

```python
import functools

import jax
import jax.numpy as jnp
from jax import lax
from jax.experimental import pallas as pl
from jax.experimental.pallas import tpu as pltpu
from jax.sharding import PartitionSpec as P

sparsity = 0.5
beta_one = 0.9
beta_two = 0.95
adam_eps = 1e-08
clip_rms = 1.0
norm_eps = 1e-06
f32 = jnp.float32
bf16 = jnp.bfloat16


def swap(value, axis, bits):
    count = lax.axis_size(axis)
    return lax.ppermute(value, axis, [(i, i ^ bits) for i in range(count)])


def adam_direction(gradient, first_part, second_part):
    new_first = first_part + (1.0 - beta_one) * gradient
    new_second = second_part + (1.0 - beta_two) * gradient * gradient
    size = new_second * lax.rsqrt(new_second) + adam_eps
    return new_first * lax.rsqrt(size * size)


def scale_kernel(count, squares_ref, enc_ref, dec_ref, enc_out, dec_out, enc_buf, dec_buf, sems):
    total = jnp.sum(squares_ref[...], keepdims=True)
    update_rms = jnp.sqrt(total / count)
    factor = 1.0 / jnp.maximum(1.0, update_rms / clip_rms)
    steps = 4
    copies = []
    for i in range(steps):
        for j, (src, buf, out) in enumerate(((enc_ref, enc_buf, enc_out), (dec_ref, dec_buf, dec_out))):
            rows = src.shape[0] // steps
            part = pl.ds(i * rows, rows)
            buf[part, :] = (src[part, :] * factor).astype(bf16)
            copy = pltpu.make_async_copy(buf.at[part, :], out.at[part, :], sems.at[i, j])
            copy.start()
            copies.append(copy)
    for copy in copies:
        copy.wait()


def scale(squares, enc_dir, dec_dir, count):
    return pl.pallas_call(
        functools.partial(scale_kernel, count),
        out_shape=(jax.ShapeDtypeStruct(enc_dir.shape, bf16), jax.ShapeDtypeStruct(dec_dir.shape, bf16)),
        in_specs=[pl.BlockSpec(memory_space=pltpu.VMEM)] * 3,
        out_specs=[pl.BlockSpec(memory_space=pl.ANY)] * 2,
        scratch_shapes=[
            pltpu.VMEM(enc_dir.shape, bf16),
            pltpu.VMEM(dec_dir.shape, bf16),
            pltpu.SemaphoreType.DMA((4, 2)),
        ],
        compiler_params=pltpu.CompilerParams(vmem_limit_bytes=24 << 20),
        name="scale_directions",
    )(squares, enc_dir, dec_dir)


def pack(value):
    top = jnp.max(jnp.abs(value), axis=-1, keepdims=True)
    level = jnp.ceil(16.0 * jnp.log2(jnp.maximum(top, 1e-30)))
    scaled = jnp.round(value * (32766.0 * jnp.exp2(level * -0.0625)))
    scaled = jnp.clip(scaled, -32766.0, 32766.0).astype(jnp.int32)
    column = lax.broadcasted_iota(jnp.int32, value.shape, value.ndim - 1)
    code = level.astype(jnp.int32) + 4096
    bit = (code >> jnp.minimum(column, 15)) & 1
    return jnp.where(column < 16, (scaled & -2) | bit, scaled).astype(jnp.int16)


def unpack(packed):
    head = packed[..., :128].astype(jnp.int32) & 1
    column = lax.broadcasted_iota(jnp.int32, head.shape, head.ndim - 1)
    code = jnp.sum(jnp.where(column < 16, head << jnp.minimum(column, 15), 0), axis=-1, keepdims=True)
    step = jnp.exp2((code - 4096).astype(f32) * 0.0625) * (1.0 / 32766.0)
    return packed.astype(f32) * step


def quad_gather(quarter):
    return [quarter] + [swap(quarter, "lat", k) for k in (1, 2, 3)]


def body(store, row_index, w_enc, decoder_matrix, m_enc, v_enc, m_dec, v_dec):
    lat_count = lax.axis_size("lat")
    high_bits = [4 << i for i in range((lat_count // 4).bit_length() - 1)]
    store = store[:, 0, :]
    w_enc, decoder_matrix, m_enc, v_enc, m_dec, v_dec = (
        a[0] for a in (w_enc, decoder_matrix, m_enc, v_enc, m_dec, v_dec)
    )
    features, latents = w_enc.shape
    own_count = row_index.shape[0]
    batch_count = own_count * lat_count
    source_count = lax.axis_size("src")
    element_count = float(batch_count * source_count * features)
    squared_error_scale = 2.0 / element_count
    sparse_scale = sparsity / element_count

    pick = row_index[:, None] == jnp.arange(store.shape[0], dtype=row_index.dtype)[None, :]
    own_rows = jnp.dot(pick.astype(bf16), store, preferred_element_type=f32).astype(bf16)
    quarter = own_rows
    for bit in high_bits:
        quarter = jnp.concatenate([quarter, swap(quarter, "lat", bit)])
    quarter_count = quarter.shape[0]
    batch_rows = jnp.concatenate(quad_gather(quarter))
    partial_value = jnp.dot(batch_rows, w_enc, preferred_element_type=f32)
    dec_wide = decoder_matrix.astype(f32)
    dec_norm = jnp.sqrt(jnp.sum(dec_wide * dec_wide, axis=1) + norm_eps)
    preact = partial_value + swap(partial_value, "src", 1)
    norm_total = dec_norm + swap(dec_norm, "src", 1)
    feature_codes = jnp.maximum(preact, 0.0).astype(bf16)
    feature_codes, m_enc, v_enc, m_dec, v_dec = lax.optimization_barrier(
        (feature_codes, m_enc, v_enc, m_dec, v_dec)
    )
    parts = jnp.dot(feature_codes, decoder_matrix, preferred_element_type=f32)
    parts = parts.reshape(4, quarter_count, features)
    total = parts[0]
    for k in (1, 2, 3):
        total = total + unpack(swap(pack(parts[k]), "lat", k))
    total, m_enc, v_enc, m_dec, v_dec = lax.optimization_barrier(
        (
            total,
            beta_one * m_enc.astype(f32),
            beta_two * v_enc.astype(f32),
            beta_one * m_dec.astype(f32),
            beta_two * v_dec.astype(f32),
        )
    )
    for at, bit in enumerate(high_bits):
        other = unpack(swap(pack(total), "lat", bit))
        span = own_count << at
        other = jnp.flip(other.reshape(-1, 2, span, features), 1).reshape(quarter_count, features)
        total = total + other
    quarter_error = (total - quarter.astype(f32)).astype(bf16)
    error_rows = jnp.concatenate(quad_gather(quarter_error))

    column_sums = jnp.sum(feature_codes.astype(f32), axis=0)
    decoder_gradient = squared_error_scale * lax.dot_general(
        feature_codes, error_rows, (((0,), (0,)), ((), ())), preferred_element_type=f32
    )
    decoder_gradient = decoder_gradient + (sparse_scale * column_sums / dec_norm)[:, None] * dec_wide
    dec_dir = adam_direction(decoder_gradient, m_dec, v_dec)
    partial_back = lax.dot_general(
        error_rows, decoder_matrix, (((1,), (1,)), ((), ())), preferred_element_type=f32
    )
    back = partial_back + swap(partial_back, "src", 1)
    pre_grad = jnp.where(
        preact > 0, squared_error_scale * back + sparse_scale * norm_total[None, :], 0.0
    ).astype(bf16)
    grad_enc = lax.dot_general(
        batch_rows, pre_grad, (((0,), (0,)), ((), ())), preferred_element_type=f32
    )
    enc_dir = adam_direction(grad_enc, m_enc, v_enc)
    squares = jnp.sum((enc_dir * enc_dir).reshape(-1, 8, 128), axis=0)
    squares = squares + jnp.sum((dec_dir * dec_dir).reshape(latents // 8, 8, -1, 128), axis=(0, 2))
    squares = squares + swap(squares, "src", 1)
    bit = 1
    while bit < lat_count:
        squares = squares + swap(squares, "lat", bit)
        bit *= 2
    enc_step, dec_step = scale(
        squares, enc_dir, dec_dir, float(2 * source_count * features * latents * lat_count)
    )
    return enc_step[None], dec_step[None]


def solution(mesh):
    return jax.shard_map(
        body,
        mesh=mesh,
        in_specs=(
            P(("grp", "lat"), "src", None),
            P(("grp", "lat")),
            P(("grp", "src"), None, "lat"),
            P(("grp", "src"), "lat", None),
            P(("grp", "src"), None, "lat"),
            P(("grp", "src"), None, "lat"),
            P(("grp", "src"), "lat", None),
            P(("grp", "src"), "lat", None),
        ),
        out_specs=(P(("grp", "src"), None, "lat"), P(("grp", "src"), "lat", None)),
        check_vma=False,
    )
```

```python
import functools

import jax
import jax.numpy as jnp
from jax import lax
from jax.experimental import pallas as pl
from jax.experimental.pallas import tpu as pltpu
from jax.sharding import PartitionSpec as P

sparsity = 0.5
beta_one = 0.9
beta_two = 0.95
adam_eps = 1e-08
clip_rms = 1.0
norm_eps = 1e-06
f32 = jnp.float32
bf16 = jnp.bfloat16
CHUNK = 512
ORDER = (1, 3, 2)


def swap(value, axis, bits):
    count = lax.axis_size(axis)
    return lax.ppermute(value, axis, [(i, i ^ bits) for i in range(count)])


def adam_direction(gradient, first_part, second_part):
    new_first = first_part + (1.0 - beta_one) * gradient
    new_second = second_part + (1.0 - beta_two) * gradient * gradient
    size = new_second * lax.rsqrt(new_second) + adam_eps
    return new_first * lax.rsqrt(size * size)


def scale_kernel(count, squares_ref, enc_ref, dec_ref, enc_out, dec_out, enc_buf, dec_buf, sems):
    total = jnp.sum(squares_ref[...], keepdims=True)
    update_rms = jnp.sqrt(total / count)
    factor = 1.0 / jnp.maximum(1.0, update_rms / clip_rms)
    steps = 4
    copies = []
    for i in range(steps):
        for j, (src, buf, out) in enumerate(((enc_ref, enc_buf, enc_out), (dec_ref, dec_buf, dec_out))):
            rows = src.shape[0] // steps
            part = pl.ds(i * rows, rows)
            buf[part, :] = (src[part, :] * factor).astype(bf16)
            copy = pltpu.make_async_copy(buf.at[part, :], out.at[part, :], sems.at[i, j])
            copy.start()
            copies.append(copy)
    for copy in copies:
        copy.wait()


def scale(squares, enc_dir, dec_dir, count):
    return pl.pallas_call(
        functools.partial(scale_kernel, count),
        out_shape=(jax.ShapeDtypeStruct(enc_dir.shape, bf16), jax.ShapeDtypeStruct(dec_dir.shape, bf16)),
        in_specs=[pl.BlockSpec(memory_space=pltpu.VMEM)] * 3,
        out_specs=[pl.BlockSpec(memory_space=pl.ANY)] * 2,
        scratch_shapes=[
            pltpu.VMEM(enc_dir.shape, bf16),
            pltpu.VMEM(dec_dir.shape, bf16),
            pltpu.SemaphoreType.DMA((4, 2)),
        ],
        compiler_params=pltpu.CompilerParams(vmem_limit_bytes=24 << 20),
        name="scale_directions",
    )(squares, enc_dir, dec_dir)


def pack(value):
    top = jnp.max(jnp.abs(value), axis=-1, keepdims=True)
    level = jnp.ceil(16.0 * jnp.log2(jnp.maximum(top, 1e-30)))
    scaled = jnp.round(value * (32766.0 * jnp.exp2(level * -0.0625)))
    scaled = jnp.clip(scaled, -32766.0, 32766.0).astype(jnp.int32)
    column = lax.broadcasted_iota(jnp.int32, value.shape, value.ndim - 1)
    code = level.astype(jnp.int32) + 4096
    bit = (code >> jnp.minimum(column, 15)) & 1
    return jnp.where(column < 16, (scaled & -2) | bit, scaled).astype(jnp.int16)


def unpack(packed):
    head = packed[..., :128].astype(jnp.int32) & 1
    column = lax.broadcasted_iota(jnp.int32, head.shape, head.ndim - 1)
    code = jnp.sum(jnp.where(column < 16, head << jnp.minimum(column, 15), 0), axis=-1, keepdims=True)
    step = jnp.exp2((code - 4096).astype(f32) * 0.0625) * (1.0 / 32766.0)
    return packed.astype(f32) * step


def row_level(top):
    return jnp.ceil(16.0 * jnp.log2(jnp.maximum(top, 1e-30)))


def store_packed(out_ref, out_rows, source, rows, level):
    scale = 32766.0 * jnp.exp2(level * -0.0625)
    width = source.shape[1]
    for at in range(0, width, CHUNK):
        part = pl.ds(at, CHUNK)
        scaled = jnp.round(source[rows, part] * scale)
        scaled = jnp.clip(scaled, -32766.0, 32766.0).astype(jnp.int32)
        if at == 0:
            column = lax.broadcasted_iota(jnp.int32, scaled.shape, 1)
            bit = ((level.astype(jnp.int32) + 4096) >> jnp.minimum(column, 15)) & 1
            scaled = jnp.where(column < 16, (scaled & -2) | bit, scaled)
        out_ref[out_rows, part] = scaled.astype(jnp.int16)


def lane_top(value):
    top = jnp.abs(value[:, :128])
    for at in range(128, value.shape[1], 128):
        top = jnp.maximum(top, jnp.abs(value[:, at : at + 128]))
    return top


def decode_kernel(own_ref, other_ref, dec_ref, codes_ref, first_ref, p1_ref, p2_ref, p3_ref, parts):
    codes = jnp.maximum(own_ref[...] + other_ref[...], 0.0).astype(bf16)
    codes_ref[...] = codes
    quarter = first_ref.shape[0]
    top = None
    for at in range(0, dec_ref.shape[1], CHUNK):
        part = pl.ds(at, CHUNK)
        value = jnp.dot(codes, dec_ref[:, part], preferred_element_type=f32)
        first_ref[:, part] = value[:quarter]
        parts[:, part] = value[quarter:]
        here = lane_top(value[quarter:])
        top = here if top is None else jnp.maximum(top, here)
    level = row_level(jnp.max(top, axis=1, keepdims=True))
    for k, out_ref in enumerate((p1_ref, p2_ref, p3_ref)):
        rows = pl.ds(k * quarter, quarter)
        store_packed(out_ref, pl.ds(0, quarter), parts, rows, level[k * quarter : (k + 1) * quarter])


def decode(own, other, dec):
    batch, latents = own.shape
    features = dec.shape[1]
    quarter = batch // 4
    packed = jax.ShapeDtypeStruct((quarter, features), jnp.int16)
    return pl.pallas_call(
        decode_kernel,
        out_shape=(
            jax.ShapeDtypeStruct((batch, latents), bf16),
            jax.ShapeDtypeStruct((quarter, features), f32),
            packed,
            packed,
            packed,
        ),
        in_specs=[pl.BlockSpec(memory_space=pltpu.VMEM)] * 3,
        out_specs=[pl.BlockSpec(memory_space=pltpu.VMEM)] * 5,
        scratch_shapes=[pltpu.VMEM((3 * quarter, features), f32)],
        compiler_params=pltpu.CompilerParams(vmem_limit_bytes=32 << 20),
        cost_estimate=pl.CostEstimate(
            flops=2 * batch * latents * features, bytes_accessed=2 * latents * features, transcendentals=0
        ),
        name="decode_and_pack",
    )(own, other, dec)


def read_step(packed_ref):
    head = packed_ref[:, :128].astype(jnp.int32) & 1
    column = lax.broadcasted_iota(jnp.int32, head.shape, 1)
    weight = jnp.where(column < 16, jnp.int32(1) << jnp.minimum(column, 15), 0)
    code = jnp.sum((head * weight).astype(f32), axis=1, keepdims=True)
    return jnp.exp2((code - 4096.0) * 0.0625) * (1.0 / 32766.0)


def quad_sum_kernel(first_ref, p1_ref, p2_ref, p3_ref, total_ref, packed_ref):
    refs = (p1_ref, p2_ref, p3_ref)
    steps = [read_step(ref) for ref in refs]
    top = None
    for at in range(0, first_ref.shape[1], CHUNK):
        part = pl.ds(at, CHUNK)
        value = first_ref[:, part]
        for ref, step in zip(refs, steps):
            value = value + ref[:, part].astype(f32) * step
        total_ref[:, part] = value
        here = lane_top(value)
        top = here if top is None else jnp.maximum(top, here)
    level = row_level(jnp.max(top, axis=1, keepdims=True))
    rows = pl.ds(0, first_ref.shape[0])
    store_packed(packed_ref, rows, total_ref, rows, level)


def quad_sum(first, received):
    return pl.pallas_call(
        quad_sum_kernel,
        out_shape=(
            jax.ShapeDtypeStruct(first.shape, f32),
            jax.ShapeDtypeStruct(first.shape, jnp.int16),
        ),
        in_specs=[pl.BlockSpec(memory_space=pltpu.VMEM)] * 4,
        out_specs=[pl.BlockSpec(memory_space=pltpu.VMEM)] * 2,
        compiler_params=pltpu.CompilerParams(vmem_limit_bytes=32 << 20),
        name="quad_sum",
    )(first, *received)


def quad_gather(quarter):
    return [quarter] + [swap(quarter, "lat", k) for k in ORDER]


def body(store, row_index, w_enc, decoder_matrix, m_enc, v_enc, m_dec, v_dec):
    lat_count = lax.axis_size("lat")
    high_bits = [4 << i for i in range((lat_count // 4).bit_length() - 1)]
    store = store[:, 0, :]
    w_enc, decoder_matrix, m_enc, v_enc, m_dec, v_dec = (
        a[0] for a in (w_enc, decoder_matrix, m_enc, v_enc, m_dec, v_dec)
    )
    features, latents = w_enc.shape
    own_count = row_index.shape[0]
    batch_count = own_count * lat_count
    source_count = lax.axis_size("src")
    element_count = float(batch_count * source_count * features)
    squared_error_scale = 2.0 / element_count
    sparse_scale = sparsity / element_count

    pick = row_index[:, None] == jnp.arange(store.shape[0], dtype=row_index.dtype)[None, :]
    own_rows = jnp.dot(pick.astype(bf16), store, preferred_element_type=f32).astype(bf16)
    quarter = own_rows
    for bit in high_bits:
        quarter = jnp.concatenate([quarter, swap(quarter, "lat", bit)])
    quarter_count = quarter.shape[0]
    batch_rows = jnp.concatenate(quad_gather(quarter))
    partial_value = jnp.dot(batch_rows, w_enc, preferred_element_type=f32)
    dec_wide = decoder_matrix.astype(f32)
    dec_norm = jnp.sqrt(jnp.sum(dec_wide * dec_wide, axis=1) + norm_eps)
    other_partial = swap(partial_value, "src", 1)
    preact = partial_value + other_partial
    feature_codes, first, *parts = decode(partial_value, other_partial, decoder_matrix)
    feature_codes, m_enc, v_enc, m_dec, v_dec = lax.optimization_barrier(
        (feature_codes, m_enc, v_enc, m_dec, v_dec)
    )
    norm_total = dec_norm + swap(dec_norm, "src", 1)
    received = [swap(part, "lat", k) for part, k in zip(parts, ORDER)]
    received[0], m_enc, v_enc, m_dec, v_dec = lax.optimization_barrier(
        (
            received[0],
            beta_one * m_enc.astype(f32),
            beta_two * v_enc.astype(f32),
            beta_one * m_dec.astype(f32),
            beta_two * v_dec.astype(f32),
        )
    )
    total, packed = quad_sum(first, received)
    for at, bit in enumerate(high_bits):
        other = unpack(swap(packed if at == 0 else pack(total), "lat", bit))
        span = own_count << at
        other = jnp.flip(other.reshape(-1, 2, span, features), 1).reshape(quarter_count, features)
        total = total + other
    quarter_error = (total - quarter.astype(f32)).astype(bf16)
    error_rows = jnp.concatenate(quad_gather(quarter_error))

    column_sums = jnp.sum(feature_codes.astype(f32), axis=0)
    decoder_gradient = squared_error_scale * lax.dot_general(
        feature_codes, error_rows, (((0,), (0,)), ((), ())), preferred_element_type=f32
    )
    decoder_gradient = decoder_gradient + (sparse_scale * column_sums / dec_norm)[:, None] * dec_wide
    dec_dir = adam_direction(decoder_gradient, m_dec, v_dec)
    partial_back = lax.dot_general(
        error_rows, decoder_matrix, (((1,), (1,)), ((), ())), preferred_element_type=f32
    )
    back = partial_back + swap(partial_back, "src", 1)
    pre_grad = jnp.where(
        preact > 0, squared_error_scale * back + sparse_scale * norm_total[None, :], 0.0
    ).astype(bf16)
    grad_enc = lax.dot_general(
        batch_rows, pre_grad, (((0,), (0,)), ((), ())), preferred_element_type=f32
    )
    enc_dir = adam_direction(grad_enc, m_enc, v_enc)
    squares = jnp.sum((enc_dir * enc_dir).reshape(-1, 8, 128), axis=0)
    squares = squares + jnp.sum((dec_dir * dec_dir).reshape(latents // 8, 8, -1, 128), axis=(0, 2))
    squares = squares + swap(squares, "src", 1)
    bit = 1
    while bit < lat_count:
        squares = squares + swap(squares, "lat", bit)
        bit *= 2
    enc_step, dec_step = scale(
        squares, enc_dir, dec_dir, float(2 * source_count * features * latents * lat_count)
    )
    return enc_step[None], dec_step[None]


def solution(mesh):
    return jax.shard_map(
        body,
        mesh=mesh,
        in_specs=(
            P(("grp", "lat"), "src", None),
            P(("grp", "lat")),
            P(("grp", "src"), None, "lat"),
            P(("grp", "src"), "lat", None),
            P(("grp", "src"), None, "lat"),
            P(("grp", "src"), None, "lat"),
            P(("grp", "src"), "lat", None),
            P(("grp", "src"), "lat", None),
        ),
        out_specs=(P(("grp", "src"), None, "lat"), P(("grp", "src"), "lat", None)),
        check_vma=False,
    )
```

```python
import functools

import jax
import jax.numpy as jnp
from jax import lax
from jax.experimental import pallas as pl
from jax.experimental.pallas import tpu as pltpu
from jax.sharding import PartitionSpec as P

sparsity = 0.5
beta_one = 0.9
beta_two = 0.95
adam_eps = 1e-08
clip_rms = 1.0
norm_eps = 1e-06
f32 = jnp.float32
bf16 = jnp.bfloat16
CHUNK = 512
ORDER = (1, 3, 2)


def swap(value, axis, bits):
    count = lax.axis_size(axis)
    return lax.ppermute(value, axis, [(i, i ^ bits) for i in range(count)])


def adam_direction(gradient, first_part, second_part):
    new_first = first_part + (1.0 - beta_one) * gradient
    new_second = second_part + (1.0 - beta_two) * gradient * gradient
    size = new_second * lax.rsqrt(new_second) + adam_eps
    return new_first * lax.rsqrt(size * size)


def scale_kernel(count, squares_ref, enc_ref, dec_ref, enc_out, dec_out, enc_buf, dec_buf, sems):
    total = jnp.sum(squares_ref[...], keepdims=True)
    update_rms = jnp.sqrt(total / count)
    factor = 1.0 / jnp.maximum(1.0, update_rms / clip_rms)
    steps = 4
    copies = []
    for i in range(steps):
        for j, (src, buf, out) in enumerate(((enc_ref, enc_buf, enc_out), (dec_ref, dec_buf, dec_out))):
            rows = src.shape[0] // steps
            part = pl.ds(i * rows, rows)
            buf[part, :] = (src[part, :] * factor).astype(bf16)
            copy = pltpu.make_async_copy(buf.at[part, :], out.at[part, :], sems.at[i, j])
            copy.start()
            copies.append(copy)
    for copy in copies:
        copy.wait()


def scale(squares, enc_dir, dec_dir, count):
    return pl.pallas_call(
        functools.partial(scale_kernel, count),
        out_shape=(jax.ShapeDtypeStruct(enc_dir.shape, bf16), jax.ShapeDtypeStruct(dec_dir.shape, bf16)),
        in_specs=[pl.BlockSpec(memory_space=pltpu.VMEM)] * 3,
        out_specs=[pl.BlockSpec(memory_space=pl.ANY)] * 2,
        scratch_shapes=[
            pltpu.VMEM(enc_dir.shape, bf16),
            pltpu.VMEM(dec_dir.shape, bf16),
            pltpu.SemaphoreType.DMA((4, 2)),
        ],
        compiler_params=pltpu.CompilerParams(vmem_limit_bytes=24 << 20),
        name="scale_directions",
    )(squares, enc_dir, dec_dir)


def pack(value):
    top = jnp.max(jnp.abs(value), axis=-1, keepdims=True)
    level = jnp.ceil(16.0 * jnp.log2(jnp.maximum(top, 1e-30)))
    scaled = jnp.round(value * (32766.0 * jnp.exp2(level * -0.0625)))
    scaled = jnp.clip(scaled, -32766.0, 32766.0).astype(jnp.int32)
    column = lax.broadcasted_iota(jnp.int32, value.shape, value.ndim - 1)
    code = level.astype(jnp.int32) + 4096
    bit = (code >> jnp.minimum(column, 15)) & 1
    return jnp.where(column < 16, (scaled & -2) | bit, scaled).astype(jnp.int16)


def unpack(packed):
    head = packed[..., :128].astype(jnp.int32) & 1
    column = lax.broadcasted_iota(jnp.int32, head.shape, head.ndim - 1)
    code = jnp.sum(jnp.where(column < 16, head << jnp.minimum(column, 15), 0), axis=-1, keepdims=True)
    step = jnp.exp2((code - 4096).astype(f32) * 0.0625) * (1.0 / 32766.0)
    return packed.astype(f32) * step


def row_level(top):
    return jnp.ceil(16.0 * jnp.log2(jnp.maximum(top, 1e-30)))


def store_packed(out_ref, out_rows, source, rows, level):
    scale = 32766.0 * jnp.exp2(level * -0.0625)
    width = source.shape[1]
    for at in range(0, width, CHUNK):
        part = pl.ds(at, CHUNK)
        scaled = jnp.round(source[rows, part] * scale)
        scaled = jnp.clip(scaled, -32766.0, 32766.0).astype(jnp.int32)
        if at == 0:
            column = lax.broadcasted_iota(jnp.int32, scaled.shape, 1)
            bit = ((level.astype(jnp.int32) + 4096) >> jnp.minimum(column, 15)) & 1
            scaled = jnp.where(column < 16, (scaled & -2) | bit, scaled)
        out_ref[out_rows, part] = scaled.astype(jnp.int16)


def lane_top(value):
    top = jnp.abs(value[:, :128])
    for at in range(128, value.shape[1], 128):
        top = jnp.maximum(top, jnp.abs(value[:, at : at + 128]))
    return top


def decode_kernel(own_ref, other_ref, dec_ref, codes_ref, first_ref, p1_ref, p2_ref, p3_ref, parts):
    codes = jnp.maximum(own_ref[...] + other_ref[...], 0.0).astype(bf16)
    codes_ref[...] = codes
    quarter = first_ref.shape[0]
    top = None
    for at in range(0, dec_ref.shape[1], CHUNK):
        part = pl.ds(at, CHUNK)
        value = jnp.dot(codes, dec_ref[:, part], preferred_element_type=f32)
        first_ref[:, part] = value[:quarter]
        parts[:, part] = value[quarter:]
        here = lane_top(value[quarter:])
        top = here if top is None else jnp.maximum(top, here)
    level = row_level(jnp.max(top, axis=1, keepdims=True))
    for k, out_ref in enumerate((p1_ref, p2_ref, p3_ref)):
        rows = pl.ds(k * quarter, quarter)
        store_packed(out_ref, pl.ds(0, quarter), parts, rows, level[k * quarter : (k + 1) * quarter])


def decode(own, other, dec):
    batch, latents = own.shape
    features = dec.shape[1]
    quarter = batch // 4
    packed = jax.ShapeDtypeStruct((quarter, features), jnp.int16)
    return pl.pallas_call(
        decode_kernel,
        out_shape=(
            jax.ShapeDtypeStruct((batch, latents), bf16),
            jax.ShapeDtypeStruct((quarter, features), f32),
            packed,
            packed,
            packed,
        ),
        in_specs=[pl.BlockSpec(memory_space=pltpu.VMEM)] * 3,
        out_specs=[pl.BlockSpec(memory_space=pltpu.VMEM)] * 5,
        scratch_shapes=[pltpu.VMEM((3 * quarter, features), f32)],
        compiler_params=pltpu.CompilerParams(vmem_limit_bytes=32 << 20),
        cost_estimate=pl.CostEstimate(
            flops=2 * batch * latents * features, bytes_accessed=2 * latents * features, transcendentals=0
        ),
        name="decode_and_pack",
    )(own, other, dec)


def read_step(packed_ref):
    head = packed_ref[:, :128].astype(jnp.int32) & 1
    column = lax.broadcasted_iota(jnp.int32, head.shape, 1)
    weight = jnp.where(column < 16, jnp.int32(1) << jnp.minimum(column, 15), 0)
    code = jnp.sum((head * weight).astype(f32), axis=1, keepdims=True)
    return jnp.exp2((code - 4096.0) * 0.0625) * (1.0 / 32766.0)


def quad_sum_kernel(first_ref, p1_ref, p2_ref, p3_ref, total_ref, packed_ref):
    refs = (p1_ref, p2_ref, p3_ref)
    steps = [read_step(ref) for ref in refs]
    top = None
    for at in range(0, first_ref.shape[1], CHUNK):
        part = pl.ds(at, CHUNK)
        value = first_ref[:, part]
        for ref, step in zip(refs, steps):
            value = value + ref[:, part].astype(f32) * step
        total_ref[:, part] = value
        here = lane_top(value)
        top = here if top is None else jnp.maximum(top, here)
    level = row_level(jnp.max(top, axis=1, keepdims=True))
    rows = pl.ds(0, first_ref.shape[0])
    store_packed(packed_ref, rows, total_ref, rows, level)


def quad_sum(first, received):
    return pl.pallas_call(
        quad_sum_kernel,
        out_shape=(
            jax.ShapeDtypeStruct(first.shape, f32),
            jax.ShapeDtypeStruct(first.shape, jnp.int16),
        ),
        in_specs=[pl.BlockSpec(memory_space=pltpu.VMEM)] * 4,
        out_specs=[pl.BlockSpec(memory_space=pltpu.VMEM)] * 2,
        compiler_params=pltpu.CompilerParams(vmem_limit_bytes=32 << 20),
        name="quad_sum",
    )(first, *received)


def quad_gather(quarter):
    return [quarter] + [swap(quarter, "lat", k) for k in ORDER]


def body(store, row_index, w_enc, decoder_matrix, m_enc, v_enc, m_dec, v_dec):
    lat_count = lax.axis_size("lat")
    high_bits = [4 << i for i in range((lat_count // 4).bit_length() - 1)]
    store = store[:, 0, :]
    w_enc, decoder_matrix, m_enc, v_enc, m_dec, v_dec = (
        a[0] for a in (w_enc, decoder_matrix, m_enc, v_enc, m_dec, v_dec)
    )
    features, latents = w_enc.shape
    own_count = row_index.shape[0]
    batch_count = own_count * lat_count
    source_count = lax.axis_size("src")
    element_count = float(batch_count * source_count * features)
    squared_error_scale = 2.0 / element_count
    sparse_scale = sparsity / element_count

    pick = row_index[:, None] == jnp.arange(store.shape[0], dtype=row_index.dtype)[None, :]
    own_rows = jnp.dot(pick.astype(bf16), store, preferred_element_type=f32).astype(bf16)
    quarter = own_rows
    for bit in high_bits:
        quarter = jnp.concatenate([quarter, swap(quarter, "lat", bit)])
    quarter_count = quarter.shape[0]
    batch_rows = jnp.concatenate(quad_gather(quarter))
    partial_value = jnp.dot(batch_rows, w_enc, preferred_element_type=f32)
    dec_wide = decoder_matrix.astype(f32)
    dec_norm = jnp.sqrt(jnp.sum(dec_wide * dec_wide, axis=1) + norm_eps)
    other_partial = swap(partial_value, "src", 1)
    preact = partial_value + other_partial
    feature_codes, first, *parts = decode(partial_value, other_partial, decoder_matrix)
    feature_codes, m_enc, v_enc, m_dec, v_dec = lax.optimization_barrier(
        (feature_codes, m_enc, v_enc, m_dec, v_dec)
    )
    norm_total = dec_norm + swap(dec_norm, "src", 1)
    received = [swap(part, "lat", k) for part, k in zip(parts, ORDER)]
    received[0], m_enc, v_enc, m_dec, v_dec = lax.optimization_barrier(
        (
            received[0],
            beta_one * m_enc.astype(f32),
            beta_two * v_enc.astype(f32),
            beta_one * m_dec.astype(f32),
            beta_two * v_dec.astype(f32),
        )
    )
    total, packed = quad_sum(first, received)
    for at, bit in enumerate(high_bits):
        other = unpack(swap(packed if at == 0 else pack(total), "lat", bit))
        span = own_count << at
        other = jnp.flip(other.reshape(-1, 2, span, features), 1).reshape(quarter_count, features)
        total = total + other
    quarter_error = (total - quarter.astype(f32)).astype(bf16)
    error_rows = jnp.concatenate(quad_gather(quarter_error))

    column_sums = jnp.sum(feature_codes.astype(f32), axis=0)
    decoder_gradient = squared_error_scale * lax.dot_general(
        feature_codes, error_rows, (((0,), (0,)), ((), ())), preferred_element_type=f32
    )
    decoder_gradient = decoder_gradient + (sparse_scale * column_sums / dec_norm)[:, None] * dec_wide
    dec_dir = adam_direction(decoder_gradient, m_dec, v_dec)
    partial_back = lax.dot_general(
        error_rows, decoder_matrix, (((1,), (1,)), ((), ())), preferred_element_type=f32
    )
    back = partial_back + swap(partial_back, "src", 1)
    pre_grad = jnp.where(
        preact > 0, squared_error_scale * back + sparse_scale * norm_total[None, :], 0.0
    ).astype(bf16)
    grad_enc = lax.dot_general(
        batch_rows, pre_grad, (((0,), (0,)), ((), ())), preferred_element_type=f32
    )
    enc_dir = adam_direction(grad_enc, m_enc, v_enc)
    squares = jnp.sum((enc_dir * enc_dir).reshape(-1, 8, 128), axis=0)
    squares = squares + jnp.sum((dec_dir * dec_dir).reshape(latents // 8, 8, -1, 128), axis=(0, 2))
    for bit in high_bits[::-1]:
        squares = squares + swap(squares, "lat", bit)
    squares = sum(swap(squares, "lat", k) for k in (3, 2, 1)) + squares
    squares = squares + swap(squares, "src", 1)
    enc_step, dec_step = scale(
        squares, enc_dir, dec_dir, float(2 * source_count * features * latents * lat_count)
    )
    return enc_step[None], dec_step[None]


def solution(mesh):
    return jax.shard_map(
        body,
        mesh=mesh,
        in_specs=(
            P(("grp", "lat"), "src", None),
            P(("grp", "lat")),
            P(("grp", "src"), None, "lat"),
            P(("grp", "src"), "lat", None),
            P(("grp", "src"), None, "lat"),
            P(("grp", "src"), None, "lat"),
            P(("grp", "src"), "lat", None),
            P(("grp", "src"), "lat", None),
        ),
        out_specs=(P(("grp", "src"), None, "lat"), P(("grp", "src"), "lat", None)),
        check_vma=False,
    )
```

```python
import functools

import jax
import jax.numpy as jnp
from jax import lax
from jax.experimental import pallas as pl
from jax.experimental.pallas import tpu as pltpu
from jax.sharding import PartitionSpec as P

sparsity = 0.5
beta_one = 0.9
beta_two = 0.95
adam_eps = 1e-08
clip_rms = 1.0
norm_eps = 1e-06
f32 = jnp.float32
bf16 = jnp.bfloat16
CHUNK = 256
ORDER = (3, 1, 2)


def swap(value, axis, bits):
    count = lax.axis_size(axis)
    return lax.ppermute(value, axis, [(i, i ^ bits) for i in range(count)])


def adam_direction(gradient, first_part, second_part):
    new_first = first_part + (1.0 - beta_one) * gradient
    new_second = second_part + (1.0 - beta_two) * gradient * gradient
    size = new_second * lax.rsqrt(new_second) + adam_eps
    return new_first * lax.rsqrt(size * size)


def scale_kernel(count, squares_ref, other_ref, enc_ref, dec_ref, enc_out, dec_out, enc_buf, dec_buf, sems):
    total = jnp.sum(squares_ref[...] + other_ref[...], keepdims=True)
    update_rms = jnp.sqrt(total / count)
    factor = 1.0 / jnp.maximum(1.0, update_rms / clip_rms)
    steps = 4
    copies = []
    for i in range(steps):
        for j, (src, buf, out) in enumerate(((enc_ref, enc_buf, enc_out), (dec_ref, dec_buf, dec_out))):
            rows = src.shape[0] // steps
            part = pl.ds(i * rows, rows)
            buf[part, :] = (src[part, :] * factor).astype(bf16)
            copy = pltpu.make_async_copy(buf.at[part, :], out.at[part, :], sems.at[i, j])
            copy.start()
            copies.append(copy)
    for copy in copies:
        copy.wait()


def scale(squares, other, enc_dir, dec_dir, count):
    return pl.pallas_call(
        functools.partial(scale_kernel, count),
        out_shape=(jax.ShapeDtypeStruct(enc_dir.shape, bf16), jax.ShapeDtypeStruct(dec_dir.shape, bf16)),
        in_specs=[pl.BlockSpec(memory_space=pltpu.VMEM)] * 4,
        out_specs=[pl.BlockSpec(memory_space=pl.ANY)] * 2,
        scratch_shapes=[
            pltpu.VMEM(enc_dir.shape, bf16),
            pltpu.VMEM(dec_dir.shape, bf16),
            pltpu.SemaphoreType.DMA((4, 2)),
        ],
        compiler_params=pltpu.CompilerParams(vmem_limit_bytes=24 << 20),
        name="scale_directions",
    )(squares, other, enc_dir, dec_dir)


def pack(value):
    top = jnp.max(jnp.abs(value), axis=-1, keepdims=True)
    level = jnp.ceil(16.0 * jnp.log2(jnp.maximum(top, 1e-30)))
    scaled = jnp.round(value * (32766.0 * jnp.exp2(level * -0.0625)))
    scaled = jnp.clip(scaled, -32766.0, 32766.0).astype(jnp.int32)
    column = lax.broadcasted_iota(jnp.int32, value.shape, value.ndim - 1)
    code = level.astype(jnp.int32) + 4096
    bit = (code >> jnp.minimum(column, 15)) & 1
    return jnp.where(column < 16, (scaled & -2) | bit, scaled).astype(jnp.int16)


def unpack(packed):
    head = packed[..., :128].astype(jnp.int32) & 1
    column = lax.broadcasted_iota(jnp.int32, head.shape, head.ndim - 1)
    code = jnp.sum(jnp.where(column < 16, head << jnp.minimum(column, 15), 0), axis=-1, keepdims=True)
    step = jnp.exp2((code - 4096).astype(f32) * 0.0625) * (1.0 / 32766.0)
    return packed.astype(f32) * step


def row_level(top):
    return jnp.ceil(16.0 * jnp.log2(jnp.maximum(top, 1e-30)))


def store_packed(out_ref, out_rows, source, rows, level):
    scale = 32766.0 * jnp.exp2(level * -0.0625)
    width = source.shape[1]
    for at in range(0, width, CHUNK):
        part = pl.ds(at, CHUNK)
        scaled = jnp.round(source[rows, part] * scale)
        scaled = jnp.clip(scaled, -32766.0, 32766.0).astype(jnp.int32)
        if at == 0:
            column = lax.broadcasted_iota(jnp.int32, scaled.shape, 1)
            bit = ((level.astype(jnp.int32) + 4096) >> jnp.minimum(column, 15)) & 1
            scaled = jnp.where(column < 16, (scaled & -2) | bit, scaled)
        out_ref[out_rows, part] = scaled.astype(jnp.int16)


def lane_top(value):
    top = jnp.abs(value[:, :128])
    for at in range(128, value.shape[1], 128):
        top = jnp.maximum(top, jnp.abs(value[:, at : at + 128]))
    return top


def decode_kernel(own_ref, other_ref, dec_ref, codes_ref, first_ref, p1_ref, p2_ref, p3_ref, parts):
    codes = jnp.maximum(own_ref[...] + other_ref[...], 0.0).astype(bf16)
    codes_ref[...] = codes
    quarter = first_ref.shape[0]
    top = None
    for at in range(0, dec_ref.shape[1], CHUNK):
        part = pl.ds(at, CHUNK)
        value = jnp.dot(codes, dec_ref[:, part], preferred_element_type=f32)
        first_ref[:, part] = value[:quarter]
        parts[:, part] = value[quarter:]
        here = lane_top(value[quarter:])
        top = here if top is None else jnp.maximum(top, here)
    level = row_level(jnp.max(top, axis=1, keepdims=True))
    for k, out_ref in enumerate((p1_ref, p2_ref, p3_ref)):
        rows = pl.ds(k * quarter, quarter)
        store_packed(out_ref, pl.ds(0, quarter), parts, rows, level[k * quarter : (k + 1) * quarter])


def decode(own, other, dec):
    batch, latents = own.shape
    features = dec.shape[1]
    quarter = batch // 4
    packed = jax.ShapeDtypeStruct((quarter, features), jnp.int16)
    return pl.pallas_call(
        decode_kernel,
        out_shape=(
            jax.ShapeDtypeStruct((batch, latents), bf16),
            jax.ShapeDtypeStruct((quarter, features), f32),
            packed,
            packed,
            packed,
        ),
        in_specs=[pl.BlockSpec(memory_space=pltpu.VMEM)] * 3,
        out_specs=[pl.BlockSpec(memory_space=pltpu.VMEM)] * 5,
        scratch_shapes=[pltpu.VMEM((3 * quarter, features), f32)],
        compiler_params=pltpu.CompilerParams(vmem_limit_bytes=32 << 20),
        cost_estimate=pl.CostEstimate(
            flops=2 * batch * latents * features, bytes_accessed=2 * latents * features, transcendentals=0
        ),
        name="decode_and_pack",
    )(own, other, dec)


def read_step(packed_ref):
    head = packed_ref[:, :128].astype(jnp.int32) & 1
    column = lax.broadcasted_iota(jnp.int32, head.shape, 1)
    weight = jnp.where(column < 16, jnp.int32(1) << jnp.minimum(column, 15), 0)
    code = jnp.sum((head * weight).astype(f32), axis=1, keepdims=True)
    return jnp.exp2((code - 4096.0) * 0.0625) * (1.0 / 32766.0)


def quad_sum_kernel(first_ref, p1_ref, p2_ref, p3_ref, total_ref, packed_ref):
    refs = (p1_ref, p2_ref, p3_ref)
    steps = [read_step(ref) for ref in refs]
    top = None
    for at in range(0, first_ref.shape[1], CHUNK):
        part = pl.ds(at, CHUNK)
        value = first_ref[:, part]
        for ref, step in zip(refs, steps):
            value = value + ref[:, part].astype(f32) * step
        total_ref[:, part] = value
        here = lane_top(value)
        top = here if top is None else jnp.maximum(top, here)
    level = row_level(jnp.max(top, axis=1, keepdims=True))
    rows = pl.ds(0, first_ref.shape[0])
    store_packed(packed_ref, rows, total_ref, rows, level)


def quad_sum(first, received):
    return pl.pallas_call(
        quad_sum_kernel,
        out_shape=(
            jax.ShapeDtypeStruct(first.shape, f32),
            jax.ShapeDtypeStruct(first.shape, jnp.int16),
        ),
        in_specs=[pl.BlockSpec(memory_space=pltpu.VMEM)] * 4,
        out_specs=[pl.BlockSpec(memory_space=pltpu.VMEM)] * 2,
        compiler_params=pltpu.CompilerParams(vmem_limit_bytes=32 << 20),
        name="quad_sum",
    )(first, *received)


def quad_gather(quarter):
    return [quarter] + [swap(quarter, "lat", k) for k in ORDER]


def body(store, row_index, w_enc, decoder_matrix, m_enc, v_enc, m_dec, v_dec):
    lat_count = lax.axis_size("lat")
    high_bits = [4 << i for i in range((lat_count // 4).bit_length() - 1)]
    store = store[:, 0, :]
    w_enc, decoder_matrix, m_enc, v_enc, m_dec, v_dec = (
        a[0] for a in (w_enc, decoder_matrix, m_enc, v_enc, m_dec, v_dec)
    )
    features, latents = w_enc.shape
    own_count = row_index.shape[0]
    batch_count = own_count * lat_count
    source_count = lax.axis_size("src")
    element_count = float(batch_count * source_count * features)
    squared_error_scale = 2.0 / element_count
    sparse_scale = sparsity / element_count

    pick = row_index[:, None] == jnp.arange(store.shape[0], dtype=row_index.dtype)[None, :]
    own_rows = jnp.dot(pick.astype(bf16), store, preferred_element_type=f32).astype(bf16)
    quarter = own_rows
    for bit in high_bits:
        quarter = jnp.concatenate([quarter, swap(quarter, "lat", bit)])
    quarter_count = quarter.shape[0]
    batch_rows = jnp.concatenate(quad_gather(quarter))
    partial_value = jnp.dot(batch_rows, w_enc, preferred_element_type=f32)
    dec_wide = decoder_matrix.astype(f32)
    dec_norm = jnp.sqrt(jnp.sum(dec_wide * dec_wide, axis=1) + norm_eps)
    other_partial = swap(partial_value, "src", 1)
    preact = partial_value + other_partial
    feature_codes, first, *parts = decode(partial_value, other_partial, decoder_matrix)
    feature_codes, m_enc, v_enc, m_dec, v_dec = lax.optimization_barrier(
        (feature_codes, m_enc, v_enc, m_dec, v_dec)
    )
    norm_total = dec_norm + swap(dec_norm, "src", 1)
    received = [swap(parts[ORDER.index(k)], "lat", k) for k in (1, 3, 2)]
    received[0], m_enc, v_enc, m_dec, v_dec = lax.optimization_barrier(
        (
            received[0],
            beta_one * m_enc.astype(f32),
            beta_two * v_enc.astype(f32),
            beta_one * m_dec.astype(f32),
            beta_two * v_dec.astype(f32),
        )
    )
    total, packed = quad_sum(first, received)
    for at, bit in enumerate(high_bits):
        other = unpack(swap(packed if at == 0 else pack(total), "lat", bit))
        span = own_count << at
        other = jnp.flip(other.reshape(-1, 2, span, features), 1).reshape(quarter_count, features)
        total = total + other
    quarter_error = (total - quarter.astype(f32)).astype(bf16)
    error_rows = jnp.concatenate(quad_gather(quarter_error))

    column_sums = jnp.sum(feature_codes.astype(f32), axis=0)
    decoder_gradient = squared_error_scale * lax.dot_general(
        feature_codes, error_rows, (((0,), (0,)), ((), ())), preferred_element_type=f32
    )
    decoder_gradient = decoder_gradient + (sparse_scale * column_sums / dec_norm)[:, None] * dec_wide
    dec_dir = adam_direction(decoder_gradient, m_dec, v_dec)
    partial_back = lax.dot_general(
        error_rows, decoder_matrix, (((1,), (1,)), ((), ())), preferred_element_type=f32
    )
    back = partial_back + swap(partial_back, "src", 1)
    pre_grad = jnp.where(
        preact > 0, squared_error_scale * back + sparse_scale * norm_total[None, :], 0.0
    ).astype(bf16)
    grad_enc = lax.dot_general(
        batch_rows, pre_grad, (((0,), (0,)), ((), ())), preferred_element_type=f32
    )
    enc_dir = adam_direction(grad_enc, m_enc, v_enc)
    squares = jnp.sum((enc_dir * enc_dir).reshape(-1, 8, 128), axis=0)
    squares = squares + jnp.sum((dec_dir * dec_dir).reshape(latents // 8, 8, -1, 128), axis=(0, 2))
    for bit in high_bits[::-1]:
        squares = squares + swap(squares, "lat", bit)
    squares = sum(swap(squares, "lat", k) for k in (3, 2, 1)) + squares
    other_squares = swap(squares, "src", 1)
    enc_step, dec_step = scale(
        squares, other_squares, enc_dir, dec_dir, float(2 * source_count * features * latents * lat_count)
    )
    return enc_step[None], dec_step[None]


def solution(mesh):
    return jax.shard_map(
        body,
        mesh=mesh,
        in_specs=(
            P(("grp", "lat"), "src", None),
            P(("grp", "lat")),
            P(("grp", "src"), None, "lat"),
            P(("grp", "src"), "lat", None),
            P(("grp", "src"), None, "lat"),
            P(("grp", "src"), None, "lat"),
            P(("grp", "src"), "lat", None),
            P(("grp", "src"), "lat", None),
        ),
        out_specs=(P(("grp", "src"), None, "lat"), P(("grp", "src"), "lat", None)),
        check_vma=False,
    )
```
